1024 devices in a mesh: dp: 16 (over y, x), expert: 64 (over z, core).
Axes of the slice: x: 4, y: 4, z: 32, core: 2. Of those that a mesh axis runs over, the one named last changes fastest.
Arguments:
- latent: bfloat16 [131072, 1024], P(('dp', 'expert')), may hold values from -6 to 6
- cotangent: bfloat16 [131072, 1024], P(('dp', 'expert')), may hold values from -0.59765625 to 0.59765625
- routes: int32 [131072, 1], P(('dp', 'expert')), may hold values from 0 to 63; in each aligned block of 128 rows (0 to 127, 128 to 255, ...) at most 4 rows name the same one
- gates: float32 [131072, 1], P(('dp', 'expert')), may hold values from 0.1 to 1
- w_in: bfloat16 [64, 1024, 2048], P('expert'), may hold values from -0.1875 to 0.1875
- w_out: bfloat16 [64, 1024, 1024], P('expert'), may hold values from -0.1875 to 0.1875
Outputs:
- output: bfloat16 [131072, 1024], P(('dp', 'expert'))
- grad_in: float32 [64, 1024, 2048], P('expert', 'dp')
- grad_out: float32 [64, 1024, 1024], P('expert', 'dp')
The draws below stay inside these ranges and needn't reach their ends.
Inputs may be any that keep to these rules, and one draw needn't show every extreme that they name: In each aligned block of 128 tokens no expert is named by more than 4 routes, a bound that some block reaches.
All inputs are finite; a program needn't handle non-finite values.
Results may differ from the reference program's by a relative error of at most 0.018.
Values may be sent and summed in bfloat16 or wider, within the bound.
No kernel may reach another device: no remote copies, remote signals or barrier semaphores. Data moves between devices by JAX's collectives and lax.ppermute only.
A program may use at most 64 MiB of HBM per device.

```python
import math
import jax
import jax.numpy as jnp
import numpy as np
from jax import lax

L = 1024
H = 1024
T_DEV = 128
TOP = 1
EXPERTS = 64
CAP = 4
TOKENS = 131072
N_DP = 16
N_EXPERT = 64


def level_of(rng, shape, cuts, low, largest):
    gain, own = 1.0, jax.random.fold_in(rng, 6)
    for axis_at, parts in cuts:
        heights = jnp.exp(jax.random.uniform(jax.random.fold_in(own, axis_at), (parts,), jnp.float32, low / len(cuts), largest / len(cuts)))
        gain = gain * jnp.repeat(heights, shape[axis_at] // parts).reshape([-1 if axis == axis_at else 1 for axis in range(len(shape))])
    return gain


def assign_block(key, own, number, rows, number_of, top, bound, lean):
    sequence = jax.random.permutation(key, number_of)
    heavy_load, common = shares(number_of, rows * top, bound, lean, True), shares(number_of, rows * top, bound, lean, False)
    places = jnp.arange(number_of)

    def named(sizes, turn):
        used = int((sizes > 0).sum())
        fixed = max(1, used // 4)
        shifted = fixed + (places - fixed + turn * (used - fixed)) % max(1, number_of - fixed)
        return jnp.zeros((number_of,), jnp.int32).at[sequence[jnp.where(places < fixed, places, shifted)]].set(jnp.asarray(sizes, jnp.int32))

    sizes = jnp.where(number % 4 == 0, named(heavy_load, number // 4), named(common, number - number // 4 - 1))
    mixed = jax.random.permutation(jax.random.fold_in(own, 3), number_of)
    donor, taker = mixed[0:number_of // 2 * 2:2], mixed[1:number_of // 2 * 2:2]
    room = jnp.minimum(sizes[donor] - 1, bound - sizes[taker]) // 2
    room = jnp.where((donor == sequence[0]) | (taker == sequence[0]) | (sizes[taker] == 0), 0, jnp.maximum(room, 0))
    shifted = jax.random.randint(jax.random.fold_in(own, 4), (number_of // 2,), 0, 1 << 20) % (room + 1)
    sizes = sizes.at[donor].add(-shifted).at[taker].add(shifted)
    members = jnp.searchsorted(jnp.cumsum(sizes), jnp.arange(rows * top), side="right").astype(jnp.int32)
    listing = members.reshape(top, rows).T
    listing = listing[jax.random.permutation(jax.random.fold_in(own, 1), rows)]
    turn = jax.random.randint(jax.random.fold_in(own, 2), (rows, 1), 0, top)
    return jnp.take_along_axis(listing, (jnp.arange(top)[None, :] + turn) % top, axis=1)


def shares(amount, total, bound, skew, full):
    loads = [(1 << 20) // math.isqrt(rank ** skew) + 1 for rank in range(1, amount + 1)]
    largest = bound if full else min(bound, max(-(-total // amount), total * loads[0] // sum(loads)))
    least = 1 if total - largest >= amount - 1 else 0
    holding, surplus = [largest] + [least] * (amount - 1), total - largest - least * (amount - 1)
    while surplus > 0:
        free = [i for i in range(1, amount) if holding[i] < largest] or [i for i in range(1, amount) if holding[i] < bound]
        pool, left = sum([loads[i] for i in free]), surplus
        for i in free:
            addition = min(bound - holding[i], max(1, left * loads[i] // pool), surplus)
            holding[i] = holding[i] + addition
            surplus = surplus - addition
    return np.array(holding)


def centred(own_key, dims, deviation, limit, split=(), held_as=jnp.bfloat16):
    result = jax.random.normal(own_key, dims, jnp.float32) * deviation
    if len(split) > 0:
        result = level_of(own_key, dims, split, -0.22, 0.18) * result
    return jnp.clip(result, min=-limit, max=limit).astype(held_as)


def setup_inputs(seed: int = 0) -> dict:
    key_list = jax.random.split(jax.random.key(seed), 7)
    latent = centred(key_list[0], (TOKENS, L), 1.0, 6.0, ((0, 1024),))
    cotangent = centred(key_list[1], (TOKENS, L), 0.1, 0.59765625, ((0, 1024),))
    routes_keys = jax.random.split(jax.random.fold_in(key_list[2], 1), TOKENS // T_DEV)
    routes_turns = jax.random.permutation(jax.random.fold_in(key_list[2], 3), TOKENS // T_DEV)
    routes = jax.vmap(lambda own, number: assign_block(jax.random.fold_in(key_list[2], 2), own, number, T_DEV, EXPERTS, TOP, CAP, 2))(routes_keys, routes_turns).reshape((TOKENS, TOP))
    gates = jnp.clip(jnp.exp(math.log(1.0) - 2.3025851 * jax.random.uniform(key_list[3], (TOKENS, TOP), jnp.float32) ** level_of(key_list[3], (TOKENS, TOP), ((0, 1024),), -0.2, 0.2)), 0.1, 1.0)
    w_in = centred(key_list[4], (EXPERTS, L, 2 * H), L ** -0.5, 0.1875, ((0, 64),))
    w_out = centred(key_list[5], (EXPERTS, L, H), H ** -0.5, 0.1875, ((0, 64),))
    return dict(latent=latent, cotangent=cotangent, routes=routes, gates=gates, w_in=w_in, w_out=w_out)


def expert_pass(x_buf, dy_buf, w_in_e, w_out_e):
    acts = jnp.dot(x_buf, w_in_e, preferred_element_type=jnp.float32)
    gate = acts[:, :H]
    upper = acts[:, H:]
    sig = jax.nn.sigmoid(gate)
    swish = gate * sig
    hidden = (swish * upper).astype(jnp.bfloat16)
    y_buf = lax.dot_general(hidden, w_out_e, (((1,), (1,)), ((), ())), preferred_element_type=jnp.float32).astype(jnp.bfloat16)
    d_hidden = jnp.dot(dy_buf, w_out_e, preferred_element_type=jnp.float32)
    d_gate = d_hidden * upper * sig * (1.0 + gate * (1.0 - sig))
    d_upper = d_hidden * swish
    d_acts = jnp.concatenate([d_gate, d_upper], axis=1).astype(jnp.bfloat16)
    xs = x_buf.reshape(N_DP, -1, L).astype(jnp.float32)
    das = d_acts.reshape(N_DP, -1, 2 * H).astype(jnp.float32)
    dys = dy_buf.reshape(N_DP, -1, L).astype(jnp.float32)
    hids = hidden.reshape(N_DP, -1, H).astype(jnp.float32)
    part_in = jnp.einsum("drl,drk->dlk", xs, das).astype(jnp.bfloat16).astype(jnp.float32)
    part_out = jnp.einsum("drl,drk->dlk", dys, hids).astype(jnp.bfloat16).astype(jnp.float32)
    return y_buf, jnp.sum(part_in, axis=0), jnp.sum(part_out, axis=0)


def reference(latent, cotangent, routes, gates, w_in, w_out):
    blocks = N_DP * N_EXPERT
    flat = routes.reshape(blocks, T_DEV * TOP)
    onehot = (flat[:, :, None] == jnp.arange(EXPERTS, dtype=jnp.int32)[None, None, :]).astype(jnp.int32)
    before = jnp.cumsum(onehot, axis=1) - onehot
    slot = jnp.sum(before * onehot, axis=2)
    position = (jnp.arange(blocks, dtype=jnp.int32)[:, None] * CAP + slot).reshape(-1)
    route_flat = routes.reshape(-1)
    gate_flat = gates.reshape(-1)
    x_rows = jnp.repeat(latent, TOP, axis=0)
    dy_rows = (gate_flat[:, None] * jnp.repeat(cotangent, TOP, axis=0).astype(jnp.float32)).astype(jnp.bfloat16)
    size = blocks * CAP

    def one_expert(expert_id):
        index = jnp.where(route_flat == expert_id, position, size).astype(jnp.int32)
        x_buf = jnp.zeros((size, L), jnp.bfloat16).at[index].set(x_rows, mode="drop")
        dy_buf = jnp.zeros((size, L), jnp.bfloat16).at[index].set(dy_rows, mode="drop")
        return expert_pass(x_buf, dy_buf, w_in[expert_id], w_out[expert_id])

    y_bufs, grad_in, grad_out = lax.map(one_expert, jnp.arange(EXPERTS, dtype=jnp.int32))
    y_rows = y_bufs[route_flat, position].astype(jnp.float32)
    output = jnp.sum((gate_flat[:, None] * y_rows).reshape(-1, TOP, L), axis=1).astype(jnp.bfloat16)
    return output, grad_in, grad_out
```

```python
import functools
import jax
import jax.numpy as jnp
from jax import lax
from jax.experimental import pallas as pl
from jax.experimental.pallas import tpu as pltpu
from jax.sharding import PartitionSpec as P

BF = jnp.bfloat16
F32 = jnp.float32
MIB = 1 << 20
RING = 4


def call(body, outs, flops, moved, n_in, scalars=0, vmem=32, scratch=()):
    vm = pl.BlockSpec(memory_space=pltpu.VMEM)
    sm = pl.BlockSpec(memory_space=pltpu.SMEM)
    return pl.pallas_call(
        body,
        out_shape=[jax.ShapeDtypeStruct(s, t) for s, t in outs],
        in_specs=[sm] * scalars + [vm] * n_in,
        out_specs=[vm] * len(outs),
        scratch_shapes=list(scratch),
        compiler_params=pltpu.CompilerParams(vmem_limit_bytes=vmem * MIB),
        cost_estimate=pl.CostEstimate(flops=flops, bytes_accessed=moved, transcendentals=0),
    )


def dot(a, b, dims):
    return lax.dot_general(a, b, (dims, ((), ())), preferred_element_type=F32)


def place_kernel(cap, x_ref, c_ref, r_ref, g_ref, send_ref, pos_ref):
    tok = x_ref.shape[0]
    r = jnp.broadcast_to(r_ref[...], (tok, tok))
    g = jnp.transpose(jnp.broadcast_to(g_ref[...], (tok, tok)))[:, :1]
    row = lax.broadcasted_iota(jnp.int32, (tok, tok), 0)
    col = lax.broadcasted_iota(jnp.int32, (tok, tok), 1)
    same = jnp.where((jnp.transpose(r) == r) & (row < col), 1, 0)
    slot = jnp.sum(same, axis=0, keepdims=True)
    route = r_ref[...]
    pos_ref[...] = route * cap + slot
    at = route * (2 * cap) + slot
    at = jnp.concatenate([at, at + cap], axis=1)
    rows = lax.broadcasted_iota(jnp.int32, (send_ref.shape[0], 2 * tok), 0)
    placing = jnp.where(rows == at, 1.0, 0.0).astype(BF)
    dy = (g * c_ref[...].astype(F32)).astype(BF)
    both = jnp.concatenate([x_ref[...], dy], axis=0)
    send_ref[...] = dot(placing, both, ((1,), (0,))).astype(BF)


def forward_kernel(cap, got_ref, wi_ref, wo_ref, y_ref, x_ref, dy_ref, hid_ref, gu_ref):
    n = x_ref.shape[0]
    hidden = wo_ref.shape[1]
    r = lax.broadcasted_iota(jnp.int32, (n, 2 * n), 0)
    c = lax.broadcasted_iota(jnp.int32, (n, 2 * n), 1)
    at = (r // cap) * (2 * cap) + r % cap
    got = got_ref[...]
    x = dot(jnp.where(c == at, 1.0, 0.0).astype(BF), got, ((1,), (0,))).astype(BF)
    x_ref[...] = x
    step = 512
    for h in range(0, hidden, step):
        g = dot(x, wi_ref[:, h : h + step], ((1,), (0,)))
        u = dot(x, wi_ref[:, hidden + h : hidden + h + step], ((1,), (0,)))
        gu_ref[:, h : h + step] = g
        gu_ref[:, hidden + h : hidden + h + step] = u
        hid_ref[:, h : h + step] = (g * jax.nn.sigmoid(g) * u).astype(BF)
    y_ref[...] = dot(hid_ref[...], wo_ref[...], ((1,), (1,))).astype(BF)
    dy_ref[...] = dot(jnp.where(c == at + cap, 1.0, 0.0).astype(BF), got, ((1,), (0,))).astype(BF)


def backward_kernel(me_ref, x_ref, dy_ref, hid_ref, gu_ref, wo_ref, *refs):
    a, b = refs[:RING], refs[RING : 2 * RING]
    da_ref, acc_ref = refs[2 * RING :]
    n, hidden = hid_ref.shape
    dy = dy_ref[...]
    step = 512
    for h in range(0, hidden, step):
        dh = dot(dy, wo_ref[:, h : h + step], ((1,), (0,)))
        g = gu_ref[:, h : h + step]
        u = gu_ref[:, hidden + h : hidden + h + step]
        sig = jax.nn.sigmoid(g)
        da_ref[:, h : h + step] = (dh * u * sig * (1.0 + g * (1.0 - sig))).astype(BF)
        da_ref[:, hidden + h : hidden + h + step] = (dh * (g * sig)).astype(BF)
    me_y, me_x = me_ref[0], me_ref[1]
    block = x_ref.shape[1] // RING
    share = block // RING
    half_in, half_out = hidden, hidden // 2

    def half(k, lhs_x, lhs_dy):
        acc_ref[:, :half_in] = dot(lhs_x, da_ref[:, k * half_in : (k + 1) * half_in], ((0,), (0,))).astype(BF)
        acc_ref[:, half_in:] = dot(lhs_dy, hid_ref[:, k * half_out : (k + 1) * half_out], ((0,), (0,))).astype(BF)

    for y in range(RING):
        cols = slice(y * block, (y + 1) * block)
        half(0, x_ref[:, cols], dy_ref[:, cols])
        for s in range(RING):
            at = pl.multiple_of(((me_x + s) % RING) * share, share)
            a[s][y] = acc_ref[pl.ds(at, share), :]
    for s in range(RING):
        at = pl.multiple_of(((me_y + s) % RING) * block, block)
        half(1, x_ref[:, pl.ds(at, block)], dy_ref[:, pl.ds(at, block)])
        for x in range(RING):
            b[s][x] = acc_ref[x * share : (x + 1) * share, :]


def middle_kernel(me_ref, *refs):
    a, b = refs[:RING], refs[RING : 2 * RING]
    a_out, b_out = refs[2 * RING : 3 * RING], refs[3 * RING :]
    for parts, outs, me in ((a, a_out, me_ref[0]), (b, b_out, me_ref[1])):
        for t in range(RING):
            at = (me + t) % RING
            total = parts[0][at].astype(F32)
            for part in parts[1:]:
                total = total + part[at].astype(F32)
            outs[t][...] = total.astype(outs[t].dtype)


def last_kernel(*refs):
    a, b = refs[:RING], refs[RING : 2 * RING]
    in_ref, out_ref = refs[2 * RING :]
    half_in, half_out = in_ref.shape[1] // 2, out_ref.shape[1] // 2
    for k, parts in enumerate((a, b)):
        total = parts[0][...]
        for part in parts[1:]:
            total = total + part[...].astype(F32)
        in_ref[:, k * half_in : (k + 1) * half_in] = total[:, :half_in]
        out_ref[:, k * half_out : (k + 1) * half_out] = total[:, half_in:]


def on_device(latent, cotangent, routes, gates, w_in, w_out):
    n_experts = lax.axis_size("expert")
    tok, width = latent.shape
    hidden = w_out.shape[2]
    cap = max(2, 2 * tok // n_experts)
    rows = n_experts * cap
    me = lax.axis_index("dp")
    me = jnp.stack([me // RING, me % RING]).astype(jnp.int32)
    gate_row = gates.reshape(1, tok)

    send, pos = call(
        functools.partial(place_kernel, cap),
        [((2 * rows, width), BF), ((1, tok), jnp.int32)],
        4 * rows * tok * width * 2, 4 * MIB, 4,
    )(latent, cotangent, routes.reshape(1, tok), gate_row)
    got = lax.all_to_all(
        send.reshape(n_experts, 2 * cap, width), "expert", split_axis=0, concat_axis=0, tiled=True
    ).reshape(2 * rows, width)

    y_buf, x_buf, dy_buf, hid, gu = call(
        functools.partial(forward_kernel, cap),
        [
            ((rows, width), BF),
            ((rows, width), BF),
            ((rows, width), BF),
            ((rows, hidden), BF),
            ((rows, 2 * hidden), F32),
        ],
        2 * rows * width * hidden * 5, 12 * MIB, 3, vmem=40,
    )(got, w_in[0], w_out[0])
    back = lax.all_to_all(
        y_buf.reshape(n_experts, cap, width), "expert", split_axis=0, concat_axis=0, tiled=True
    ).reshape(rows, width)

    share = width // (RING * RING)
    cols = hidden + hidden // 2
    parts = call(
        backward_kernel,
        [((RING, share, cols), BF)] * (2 * RING),
        2 * rows * width * hidden * 4, 16 * MIB, 5, scalars=1, vmem=40,
        scratch=[pltpu.VMEM((rows, 2 * hidden), BF), pltpu.VMEM((width // RING, cols), BF)],
    )(me, x_buf, dy_buf, hid, gu, w_out[0])

    ring = range(RING)

    def along_x(v, s):
        return lax.ppermute(v, "dp", [(RING * y + x, RING * y + (x + s) % RING) for y in ring for x in ring])

    def along_y(v, s):
        return lax.ppermute(v, "dp", [(RING * y + x, RING * ((y + s) % RING) + x) for y in ring for x in ring])

    a, b = parts[:RING], parts[RING:]
    a = [a[0]] + [along_x(a[s], s) for s in (1, 2, 3)]
    b = [b[0]] + [along_y(b[s], s) for s in (1, 2, 3)]
    mids = call(
        middle_kernel,
        ([((share, cols), F32)] + [((share, cols), BF)] * (RING - 1)) * 2,
        16 * MIB, 10 * MIB, 2 * RING, scalars=1,
    )(me, *a, *b)
    a, b = mids[:RING], mids[RING:]
    a = [a[0]] + [along_y(a[s], s) for s in (1, 2, 3)]
    b = [b[0]] + [along_x(b[s], s) for s in (1, 2, 3)]
    grad_in, grad_out = call(
        last_kernel,
        [((share, 2 * hidden), F32), ((share, hidden), F32)],
        4 * MIB, 4 * MIB, 2 * RING,
    )(*a, *b)

    placing = (jnp.arange(rows, dtype=jnp.int32)[:, None] == pos).astype(BF)
    y_rows = dot(placing, back, ((0,), (0,)))
    output = (gates * y_rows).astype(BF)
    return output, grad_in[None], grad_out[None]


def solution(mesh):
    tokens = P(("dp", "expert"), None)
    return jax.shard_map(
        on_device,
        mesh=mesh,
        in_specs=(tokens,) * 4 + (P("expert", None, None),) * 2,
        out_specs=(tokens, P("expert", "dp", None), P("expert", "dp", None)),
        check_vma=False,
    )
```

```python
import functools
import jax
import jax.numpy as jnp
from jax import lax
from jax.experimental import pallas as pl
from jax.experimental.pallas import tpu as pltpu
from jax.sharding import PartitionSpec as P

BF = jnp.bfloat16
F32 = jnp.float32
MIB = 1 << 20
RING = 4


def call(body, outs, flops, moved, n_in, vmem=12, scratch=(), hbm=0, out_hbm=False):
    vm = pl.BlockSpec(memory_space=pltpu.VMEM)
    far = pl.BlockSpec(memory_space=pltpu.HBM)
    return pl.pallas_call(
        body,
        out_shape=[jax.ShapeDtypeStruct(s, t) for s, t in outs],
        in_specs=[far] * hbm + [vm] * (n_in - hbm),
        out_specs=[far if out_hbm else vm] * len(outs),
        scratch_shapes=list(scratch),
        compiler_params=pltpu.CompilerParams(vmem_limit_bytes=vmem * MIB),
        cost_estimate=pl.CostEstimate(flops=flops, bytes_accessed=moved, transcendentals=0),
    )


def dot(a, b, dims):
    return lax.dot_general(a, b, (dims, ((), ())), preferred_element_type=F32)


def place_kernel(cap, x_hbm, c_hbm, r_hbm, g_hbm, send_ref, pos_ref, x_ref, c_ref, r_ref, g_ref, sems):
    pairs = ((r_hbm, r_ref), (g_hbm, g_ref), (x_hbm, x_ref), (c_hbm, c_ref))
    copies = [pltpu.make_async_copy(a, b, sems.at[i]) for i, (a, b) in enumerate(pairs)]
    for copy in copies:
        copy.start()
    for copy in copies:
        copy.wait()
    tok = x_ref.shape[0]
    r = jnp.broadcast_to(r_ref[...], (tok, tok))
    g = jnp.transpose(jnp.broadcast_to(g_ref[...], (tok, tok)))[:, :1]
    row = lax.broadcasted_iota(jnp.int32, (tok, tok), 0)
    col = lax.broadcasted_iota(jnp.int32, (tok, tok), 1)
    same = jnp.where((jnp.transpose(r) == r) & (row < col), 1, 0)
    slot = jnp.sum(same, axis=0, keepdims=True)
    route = r_ref[...]
    pos_ref[...] = route * cap + slot
    at = route * (2 * cap) + slot
    at = jnp.concatenate([at, at + cap], axis=1)
    rows = lax.broadcasted_iota(jnp.int32, (send_ref.shape[0], 2 * tok), 0)
    placing = jnp.where(rows == at, 1.0, 0.0).astype(BF)
    dy = (g * c_ref[...].astype(F32)).astype(BF)
    both = jnp.concatenate([x_ref[...], dy], axis=0)
    send_ref[...] = dot(placing, both, ((1,), (0,))).astype(BF)


STEP = 512


def weight_copies(wi_hbm, wo_hbm, wi_ref, wo_ref, sems):
    hidden = wo_hbm.shape[1]
    pieces = [pl.ds(at, STEP) for h in range(0, hidden, STEP) for at in (h, hidden + h)]
    copies = [
        pltpu.make_async_copy(wi_hbm.at[:, cols], wi_ref.at[:, cols], sems.at[i])
        for i, cols in enumerate(pieces)
    ]
    last = pltpu.make_async_copy(wo_hbm, wo_ref, sems.at[len(copies)])
    for copy in copies:
        copy.start()
    last.start()
    return copies, last


def expert_kernel(cap, wi_hbm, wo_hbm, got_hbm, y_hbm, *refs):
    a, b = refs[:RING], refs[RING : 2 * RING]
    wi_ref, wo_ref, got_ref, y_ref, hid_ref, da_ref, acc_ref, w_sems, sems, out_sems = refs[2 * RING :]
    arrival = pltpu.make_async_copy(got_hbm, got_ref, sems.at[0])
    arrival.start()
    copies, last = weight_copies(wi_hbm, wo_hbm, wi_ref, wo_ref, w_sems)
    n, hidden = hid_ref.shape
    r = lax.broadcasted_iota(jnp.int32, (n, 2 * n), 0)
    c = lax.broadcasted_iota(jnp.int32, (n, 2 * n), 1)
    at = (r // cap) * (2 * cap) + r % cap
    arrival.wait()
    got = got_ref[...]
    x = dot(jnp.where(c == at, 1.0, 0.0).astype(BF), got, ((1,), (0,))).astype(BF)
    dy = dot(jnp.where(c == at + cap, 1.0, 0.0).astype(BF), got, ((1,), (0,))).astype(BF)
    for h in range(0, hidden, STEP):
        copies[2 * h // STEP].wait()
        g = dot(x, wi_ref[:, h : h + STEP], ((1,), (0,)))
        copies[2 * h // STEP + 1].wait()
        u = dot(x, wi_ref[:, hidden + h : hidden + h + STEP], ((1,), (0,)))
        sig = jax.nn.sigmoid(g)
        swish = g * sig
        hid_ref[:, h : h + STEP] = (swish * u).astype(BF)
        if h == 0:
            last.wait()
        dh = dot(dy, wo_ref[:, h : h + STEP], ((1,), (0,)))
        da_ref[:, h : h + STEP] = (dh * u * sig * (1.0 + g * (1.0 - sig))).astype(BF)
        da_ref[:, hidden + h : hidden + h + STEP] = (dh * swish).astype(BF)
    y = dot(hid_ref[...], wo_ref[...], ((1,), (1,)))
    y_ref[...] = y.reshape(y_ref.shape).astype(BF)
    outs = [pltpu.make_async_copy(y_ref, y_hbm, sems.at[1])]
    outs[0].start()
    x_t, dy_t = jnp.transpose(x), jnp.transpose(dy)
    me = lax.axis_index("dp")
    me_y, me_x = me // RING, me % RING
    block = x.shape[1] // RING
    share = block // RING
    cols = hidden + hidden // 2
    for y_at in range(RING):
        rows = slice(y_at * block, (y_at + 1) * block)
        for k in range(2):
            acc_ref[y_at, :, k * cols : k * cols + hidden] = dot(
                x_t[rows], da_ref[:, k * hidden : (k + 1) * hidden], ((1,), (0,))
            ).astype(BF)
            acc_ref[y_at, :, k * cols + hidden : (k + 1) * cols] = dot(
                dy_t[rows], hid_ref[:, k * hidden // 2 : (k + 1) * hidden // 2], ((1,), (0,))
            ).astype(BF)
        for k in range(RING):
            at = pl.multiple_of(((me_x + k) % RING) * share, share)
            outs.append(
                pltpu.make_async_copy(
                    acc_ref.at[y_at, pl.ds(at, share), pl.ds(0, cols)],
                    a[k].at[y_at],
                    out_sems.at[0, y_at, k],
                )
            )
            outs[-1].start()
    for k in range(RING):
        at = (me_y + k) % RING
        for x_at in range(RING):
            outs.append(
                pltpu.make_async_copy(
                    acc_ref.at[at, pl.ds(x_at * share, share), pl.ds(cols, cols)],
                    b[k].at[x_at],
                    out_sems.at[1, k, x_at],
                )
            )
            outs[-1].start()
    for copy in outs:
        copy.wait()


def middle_kernel(axis, *refs):
    parts, outs = refs[:RING], refs[RING:]
    me = lax.axis_index("dp")
    me = me // RING if axis == 0 else me % RING
    for t in range(RING):
        at = (me + t) % RING
        total = parts[0][at].astype(F32)
        for part in parts[1:]:
            total = total + part[at].astype(F32)
        outs[t][...] = total.astype(outs[t].dtype)


def last_kernel(*refs):
    a, b = refs[:RING], refs[RING : 2 * RING]
    in_ref, out_ref = refs[2 * RING :]
    half_in, half_out = in_ref.shape[1] // 2, out_ref.shape[1] // 2
    for k, parts in enumerate((a, b)):
        total = parts[0][...]
        for part in parts[1:]:
            total = total + part[...].astype(F32)
        in_ref[:, k * half_in : (k + 1) * half_in] = total[:, :half_in]
        out_ref[:, k * half_out : (k + 1) * half_out] = total[:, half_in:]


def output_kernel(back_ref, pos_ref, g_ref, out_ref):
    tok = out_ref.shape[0]
    experts, cap, width = back_ref.shape
    g = jnp.transpose(jnp.broadcast_to(g_ref[...], (tok, tok)))[:, :1]
    rows = lax.broadcasted_iota(jnp.int32, (experts * cap, tok), 0)
    placing = jnp.where(rows == pos_ref[...], 1.0, 0.0).astype(BF)
    back = back_ref[...].astype(F32).reshape(experts * cap, width).astype(BF)
    out_ref[...] = (g * dot(placing, back, ((0,), (0,)))).astype(BF)


def on_device(latent, cotangent, routes, gates, w_in, w_out):
    n_experts = lax.axis_size("expert")
    tok, width = latent.shape
    hidden = w_out.shape[2]
    cap = max(2, 2 * tok // n_experts)
    rows = n_experts * cap
    gate_row = gates.reshape(1, tok)

    send, pos = call(
        functools.partial(place_kernel, cap),
        [((2 * rows, width), BF), ((1, tok), jnp.int32)],
        4 * rows * tok * width * 2, 4 * MIB, 4, hbm=4, vmem=62,
        scratch=[
            pltpu.VMEM((tok, width), BF),
            pltpu.VMEM((tok, width), BF),
            pltpu.VMEM((1, tok), jnp.int32),
            pltpu.VMEM((1, tok), F32),
            pltpu.SemaphoreType.DMA((4,)),
        ],
    )(latent, cotangent, routes.reshape(1, tok), gate_row)
    got = lax.all_to_all(
        send.reshape(n_experts, 2 * cap, width), "expert", split_axis=0, concat_axis=0, tiled=True
    ).reshape(2 * rows, width)

    share = width // (RING * RING)
    cols = hidden + hidden // 2
    y_buf, *parts = call(
        functools.partial(expert_kernel, cap),
        [((n_experts, cap, width), BF)] + [((RING, share, cols), BF)] * (2 * RING),
        2 * rows * width * hidden * 8, 16 * MIB, 3, hbm=3, vmem=58, out_hbm=True,
        scratch=[
            pltpu.VMEM((width, 2 * hidden), BF),
            pltpu.VMEM((width, hidden), BF),
            pltpu.VMEM((2 * rows, width), BF),
            pltpu.VMEM((n_experts, cap, width), BF),
            pltpu.VMEM((rows, hidden), BF),
            pltpu.VMEM((rows, 2 * hidden), BF),
            pltpu.VMEM((RING, width // RING, 2 * cols), BF),
            pltpu.SemaphoreType.DMA((2 * hidden // STEP + 1,)),
            pltpu.SemaphoreType.DMA((2,)),
            pltpu.SemaphoreType.DMA((2, RING, RING)),
        ],
    )(w_in[0], w_out[0], got)
    back = lax.all_to_all(y_buf, "expert", split_axis=0, concat_axis=0, tiled=True)

    def shift(v, dy, dx):
        ring = range(RING)
        pairs = [
            (RING * y + x, RING * ((y + dy) % RING) + (x + dx) % RING) for y in ring for x in ring
        ]
        return lax.ppermute(v, "dp", pairs)

    a, b = parts[:RING], parts[RING:]
    for k in range(1, RING):
        a[k] = shift(a[k], 0, k)
        b[k] = shift(b[k], k, 0)
    sums = [((share, cols), F32)] + [((share, cols), BF)] * (RING - 1)
    ends = []
    for axis, half in enumerate((a, b)):
        mids = call(
            functools.partial(middle_kernel, axis), sums, 8 * MIB, 5 * MIB, RING
        )(half[0], half[2], half[1], half[3])
        far = [shift(mids[t], t, 0) if axis == 0 else shift(mids[t], 0, t) for t in (1, 2, 3)]
        ends += [mids[0]] + far
    grad_in, grad_out = call(
        last_kernel,
        [((share, 2 * hidden), F32), ((share, hidden), F32)],
        4 * MIB, 4 * MIB, 2 * RING,
    )(*ends)

    (output,) = call(
        output_kernel, [((tok, width), BF)], 2 * rows * tok * width, MIB, 3
    )(back, pos, gate_row)
    return output, grad_in[None], grad_out[None]


def solution(mesh):
    tokens = P(("dp", "expert"), None)
    return jax.shard_map(
        on_device,
        mesh=mesh,
        in_specs=(tokens,) * 4 + (P("expert", None, None),) * 2,
        out_specs=(tokens, P("expert", "dp", None), P("expert", "dp", None)),
        check_vma=False,
    )
```

```python
import functools
import jax
import jax.numpy as jnp
from jax import lax
from jax.experimental import pallas as pl
from jax.experimental.pallas import tpu as pltpu
from jax.sharding import PartitionSpec as P

BF = jnp.bfloat16
F32 = jnp.float32
MIB = 1 << 20
RING = 4


def call(body, outs, flops, moved, n_in, vmem=12, scratch=(), hbm=0, out_hbm=False):
    vm = pl.BlockSpec(memory_space=pltpu.VMEM)
    far = pl.BlockSpec(memory_space=pltpu.HBM)
    return pl.pallas_call(
        body,
        out_shape=[jax.ShapeDtypeStruct(s, t) for s, t in outs],
        in_specs=[far] * hbm + [vm] * (n_in - hbm),
        out_specs=[far if out_hbm else vm] * len(outs),
        scratch_shapes=list(scratch),
        compiler_params=pltpu.CompilerParams(vmem_limit_bytes=vmem * MIB),
        cost_estimate=pl.CostEstimate(flops=flops, bytes_accessed=moved, transcendentals=0),
    )


def dot(a, b, dims):
    return lax.dot_general(a, b, (dims, ((), ())), preferred_element_type=F32)


def place_kernel(cap, x_hbm, c_hbm, r_hbm, g_hbm, send_ref, pos_ref, x_ref, c_ref, r_ref, g_ref, sems):
    pairs = ((r_hbm, r_ref), (g_hbm, g_ref), (x_hbm, x_ref), (c_hbm, c_ref))
    copies = [pltpu.make_async_copy(a, b, sems.at[i]) for i, (a, b) in enumerate(pairs)]
    for copy in copies:
        copy.start()
    for copy in copies:
        copy.wait()
    tok = x_ref.shape[0]
    r = jnp.broadcast_to(r_ref[...], (tok, tok))
    g = jnp.transpose(jnp.broadcast_to(g_ref[...], (tok, tok)))[:, :1]
    row = lax.broadcasted_iota(jnp.int32, (tok, tok), 0)
    col = lax.broadcasted_iota(jnp.int32, (tok, tok), 1)
    same = jnp.where((jnp.transpose(r) == r) & (row < col), 1, 0)
    slot = jnp.sum(same, axis=0, keepdims=True)
    route = r_ref[...]
    pos_ref[...] = route * cap + slot
    at = route * (2 * cap) + slot
    at = jnp.concatenate([at, at + cap], axis=1)
    rows = lax.broadcasted_iota(jnp.int32, (send_ref.shape[0], 2 * tok), 0)
    placing = jnp.where(rows == at, 1.0, 0.0).astype(BF)
    dy = (g * c_ref[...].astype(F32)).astype(BF)
    both = jnp.concatenate([x_ref[...], dy], axis=0)
    send_ref[...] = dot(placing, both, ((1,), (0,))).astype(BF)


STEP = 512


def weight_copies(wi_hbm, wo_hbm, wi_ref, wo_ref, sems):
    hidden = wo_hbm.shape[1]
    pieces = [pl.ds(at, STEP) for h in range(0, hidden, STEP) for at in (h, hidden + h)]
    copies = [
        pltpu.make_async_copy(wi_hbm.at[:, cols], wi_ref.at[:, cols], sems.at[i])
        for i, cols in enumerate(pieces)
    ]
    last = pltpu.make_async_copy(wo_hbm, wo_ref, sems.at[len(copies)])
    return copies, last


def expert_kernel(cap, wi_hbm, wo_hbm, got_hbm, y_hbm, *refs):
    a, b = refs[:RING], refs[RING : 2 * RING]
    wi_ref, wo_ref, got_ref, y_ref, hid_ref, da_ref, xt_ref, dyt_ref, acc_ref, w_sems, sems, out_sems = refs[2 * RING :]
    arrival = pltpu.make_async_copy(got_hbm, got_ref, sems.at[0])
    arrival.start()
    copies, last = weight_copies(wi_hbm, wo_hbm, wi_ref, wo_ref, w_sems)
    copies[0].start()
    copies[1].start()
    n, hidden = hid_ref.shape
    r = lax.broadcasted_iota(jnp.int32, (n, 1), 0)
    c = lax.broadcasted_iota(jnp.int32, (n, 2 * n), 1)
    at = (r // cap) * (2 * cap) + r % cap
    arrival.wait()
    last.start()
    for copy in copies[2:]:
        copy.start()
    got = got_ref[...]
    x = dot(jnp.where(c == at, 1.0, 0.0).astype(BF), got, ((1,), (0,))).astype(BF)
    dy = dot(jnp.where(c == at + cap, 1.0, 0.0).astype(BF), got, ((1,), (0,))).astype(BF)
    for h in range(0, hidden, STEP):
        copies[2 * h // STEP].wait()
        g = dot(x, wi_ref[:, h : h + STEP], ((1,), (0,)))
        copies[2 * h // STEP + 1].wait()
        u = dot(x, wi_ref[:, hidden + h : hidden + h + STEP], ((1,), (0,)))
        sig = jax.nn.sigmoid(g)
        swish = g * sig
        hid_ref[:, h : h + STEP] = (swish * u).astype(BF)
        if h == 0:
            last.wait()
        dh = dot(dy, wo_ref[:, h : h + STEP], ((1,), (0,)))
        da_ref[:, h : h + STEP] = (dh * u * sig * (1.0 + g * (1.0 - sig))).astype(BF)
        da_ref[:, hidden + h : hidden + h + STEP] = (dh * swish).astype(BF)
    y = dot(hid_ref[...], wo_ref[...], ((1,), (1,)))
    y_ref[...] = y.reshape(y_ref.shape).astype(BF)
    outs = [pltpu.make_async_copy(y_ref, y_hbm, sems.at[1])]
    outs[0].start()
    xt_ref[...] = jnp.transpose(x)
    dyt_ref[...] = jnp.transpose(dy)
    me = lax.axis_index("dp")
    me_y, me_x = me // RING, me % RING
    block = x.shape[1] // RING
    share = block // RING
    cols = hidden + hidden // 2
    for j in range(RING):
        y_at = (me_y + j) % RING
        rows = pl.ds(pl.multiple_of(y_at * block, block), block)
        for half, pieces in enumerate((a, b)):
            acc_ref[j, :, half * cols : half * cols + hidden] = dot(
                xt_ref[rows, :], da_ref[:, half * hidden : (half + 1) * hidden], ((1,), (0,))
            ).astype(BF)
            acc_ref[j, :, half * cols + hidden : (half + 1) * cols] = dot(
                dyt_ref[rows, :], hid_ref[:, half * hidden // 2 : (half + 1) * hidden // 2], ((1,), (0,))
            ).astype(BF)
            for k in range(RING):
                if half == 0:
                    at = pl.multiple_of(((me_x + k) % RING) * share, share)
                    target = a[k].at[y_at]
                else:
                    at = k * share
                    target = b[j].at[k]
                source = acc_ref.at[j, pl.ds(at, share), pl.ds(half * cols, cols)]
                outs.append(pltpu.make_async_copy(source, target, out_sems.at[half, j, k]))
                outs[-1].start()
    for copy in outs:
        copy.wait()


def middle_kernel(axis, *refs):
    parts, outs = refs[:RING], refs[RING:]
    me = lax.axis_index("dp")
    me = me // RING if axis == 0 else me % RING
    for t in range(RING):
        at = (me + t) % RING
        total = parts[0][at].astype(F32)
        for part in parts[1:]:
            total = total + part[at].astype(F32)
        outs[t][...] = total.astype(outs[t].dtype)


def last_kernel(*refs):
    a, b = refs[:RING], refs[RING : 2 * RING]
    in_ref, out_ref = refs[2 * RING :]
    half_in, half_out = in_ref.shape[1] // 2, out_ref.shape[1] // 2
    for k, parts in enumerate((a, b)):
        total = parts[0][...]
        for part in parts[1:]:
            total = total + part[...].astype(F32)
        in_ref[:, k * half_in : (k + 1) * half_in] = total[:, :half_in]
        out_ref[:, k * half_out : (k + 1) * half_out] = total[:, half_in:]


def output_kernel(back_ref, pos_ref, g_ref, out_ref):
    tok = out_ref.shape[0]
    experts, cap, width = back_ref.shape
    g = jnp.transpose(jnp.broadcast_to(g_ref[...], (tok, tok)))[:, :1]
    rows = lax.broadcasted_iota(jnp.int32, (experts * cap, tok), 0)
    placing = jnp.where(rows == pos_ref[...], 1.0, 0.0).astype(BF)
    back = back_ref[...].astype(F32).reshape(experts * cap, width).astype(BF)
    out_ref[...] = (g * dot(placing, back, ((0,), (0,)))).astype(BF)


def on_device(latent, cotangent, routes, gates, w_in, w_out):
    n_experts = lax.axis_size("expert")
    tok, width = latent.shape
    hidden = w_out.shape[2]
    cap = max(2, 2 * tok // n_experts)
    rows = n_experts * cap
    gate_row = gates.reshape(1, tok)

    send, pos = call(
        functools.partial(place_kernel, cap),
        [((2 * rows, width), BF), ((1, tok), jnp.int32)],
        4 * rows * tok * width * 2, 4 * MIB, 4, hbm=4, vmem=62,
        scratch=[
            pltpu.VMEM((tok, width), BF),
            pltpu.VMEM((tok, width), BF),
            pltpu.VMEM((1, tok), jnp.int32),
            pltpu.VMEM((1, tok), F32),
            pltpu.SemaphoreType.DMA((4,)),
        ],
    )(latent, cotangent, routes.reshape(1, tok), gate_row)
    got = lax.all_to_all(
        send.reshape(n_experts, 2 * cap, width), "expert", split_axis=0, concat_axis=0, tiled=True
    ).reshape(2 * rows, width)

    share = width // (RING * RING)
    cols = hidden + hidden // 2
    y_buf, *parts = call(
        functools.partial(expert_kernel, cap),
        [((n_experts, cap, width), BF)] + [((RING, share, cols), BF)] * (2 * RING),
        2 * rows * width * hidden * 8, 16 * MIB, 3, hbm=3, vmem=58, out_hbm=True,
        scratch=[
            pltpu.VMEM((width, 2 * hidden), BF),
            pltpu.VMEM((width, hidden), BF),
            pltpu.VMEM((2 * rows, width), BF),
            pltpu.VMEM((n_experts, cap, width), BF),
            pltpu.VMEM((rows, hidden), BF),
            pltpu.VMEM((rows, 2 * hidden), BF),
            pltpu.VMEM((width, rows), BF),
            pltpu.VMEM((width, rows), BF),
            pltpu.VMEM((RING, width // RING, 2 * cols), BF),
            pltpu.SemaphoreType.DMA((2 * hidden // STEP + 1,)),
            pltpu.SemaphoreType.DMA((2,)),
            pltpu.SemaphoreType.DMA((2, RING, RING)),
        ],
    )(w_in[0], w_out[0], got)
    back = lax.all_to_all(y_buf, "expert", split_axis=0, concat_axis=0, tiled=True)

    def shift(v, dy, dx):
        ring = range(RING)
        pairs = [
            (RING * y + x, RING * ((y + dy) % RING) + (x + dx) % RING) for y in ring for x in ring
        ]
        return lax.ppermute(v, "dp", pairs)

    a, b = parts[:RING], parts[RING:]
    for k in range(1, RING):
        a[k] = shift(a[k], 0, k)
        b[k] = shift(b[k], k, 0)
    sums = [((share, cols), F32)] + [((share, cols), BF)] * (RING - 1)
    ends = []
    for axis, half in enumerate((a, b)):
        mids = call(
            functools.partial(middle_kernel, axis), sums, 8 * MIB, 5 * MIB, RING
        )(half[0], half[2], half[1], half[3])
        far = [shift(mids[t], t, 0) if axis == 0 else shift(mids[t], 0, t) for t in (2, 1, 3)]
        ends += [mids[0]] + far
    grad_in, grad_out = call(
        last_kernel,
        [((share, 2 * hidden), F32), ((share, hidden), F32)],
        4 * MIB, 4 * MIB, 2 * RING,
    )(*ends)

    (output,) = call(
        output_kernel, [((tok, width), BF)], 2 * rows * tok * width, MIB, 3
    )(back, pos, gate_row)
    return output, grad_in[None], grad_out[None]


def solution(mesh):
    tokens = P(("dp", "expert"), None)
    return jax.shard_map(
        on_device,
        mesh=mesh,
        in_specs=(tokens,) * 4 + (P("expert", None, None),) * 2,
        out_specs=(tokens, P("expert", "dp", None), P("expert", "dp", None)),
        check_vma=False,
    )
```

```python
import functools
import jax
import jax.numpy as jnp
from jax import lax
from jax.experimental import pallas as pl
from jax.experimental.pallas import tpu as pltpu
from jax.sharding import PartitionSpec as P

BF = jnp.bfloat16
F32 = jnp.float32
MIB = 1 << 20
RING = 4


def call(body, outs, flops, moved, n_in, vmem=12, scratch=(), hbm=0, out_hbm=False):
    vm = pl.BlockSpec(memory_space=pltpu.VMEM)
    far = pl.BlockSpec(memory_space=pltpu.HBM)
    return pl.pallas_call(
        body,
        out_shape=[jax.ShapeDtypeStruct(s, t) for s, t in outs],
        in_specs=[far] * hbm + [vm] * (n_in - hbm),
        out_specs=[far if out_hbm else vm] * len(outs),
        scratch_shapes=list(scratch),
        compiler_params=pltpu.CompilerParams(vmem_limit_bytes=vmem * MIB),
        cost_estimate=pl.CostEstimate(flops=flops, bytes_accessed=moved, transcendentals=0),
    )


def dot(a, b, dims):
    return lax.dot_general(a, b, (dims, ((), ())), preferred_element_type=F32)


def place_kernel(cap, x_hbm, c_hbm, r_hbm, g_hbm, send_ref, pos_ref, x_ref, c_ref, r_ref, g_ref, sems):
    pairs = ((r_hbm, r_ref), (g_hbm, g_ref), (x_hbm, x_ref), (c_hbm, c_ref))
    copies = [pltpu.make_async_copy(a, b, sems.at[i]) for i, (a, b) in enumerate(pairs)]
    for copy in copies:
        copy.start()
    for copy in copies:
        copy.wait()
    tok = x_ref.shape[0]
    r = jnp.broadcast_to(r_ref[...], (tok, tok))
    g = jnp.transpose(jnp.broadcast_to(g_ref[...], (tok, tok)))[:, :1]
    row = lax.broadcasted_iota(jnp.int32, (tok, tok), 0)
    col = lax.broadcasted_iota(jnp.int32, (tok, tok), 1)
    same = jnp.where((jnp.transpose(r) == r) & (row < col), 1, 0)
    slot = jnp.sum(same, axis=0, keepdims=True)
    route = r_ref[...]
    pos_ref[...] = route * cap + slot
    at = route * (2 * cap) + slot
    at = jnp.concatenate([at, at + cap], axis=1)
    rows = lax.broadcasted_iota(jnp.int32, (send_ref.shape[0], 2 * tok), 0)
    placing = jnp.where(rows == at, 1.0, 0.0).astype(BF)
    dy = (g * c_ref[...].astype(F32)).astype(BF)
    both = jnp.concatenate([x_ref[...], dy], axis=0)
    send_ref[...] = dot(placing, both, ((1,), (0,))).astype(BF)


STEP = 512


def weight_copies(wi_hbm, wo_hbm, wi_ref, wo_ref, sems):
    hidden = wo_hbm.shape[1]
    pieces = [pl.ds(at, STEP) for h in range(0, hidden, STEP) for at in (h, hidden + h)]
    copies = [
        pltpu.make_async_copy(wi_hbm.at[:, cols], wi_ref.at[:, cols], sems.at[i])
        for i, cols in enumerate(pieces)
    ]
    last = pltpu.make_async_copy(wo_hbm, wo_ref, sems.at[len(copies)])
    return copies, last


def half_columns(hidden):
    few = 3 * hidden // 8
    return few, hidden - few


def expert_kernel(cap, wi_hbm, wo_hbm, got_hbm, y_hbm, *refs):
    a, b = refs[:RING], refs[RING : 2 * RING]
    wi_ref, wo_ref, got_ref, y_ref, hid_ref, da_ref, xt_ref, dyt_ref, acc_ref, w_sems, sems, out_sems = refs[2 * RING :]
    arrival = pltpu.make_async_copy(got_hbm, got_ref, sems.at[0])
    arrival.start()
    copies, last = weight_copies(wi_hbm, wo_hbm, wi_ref, wo_ref, w_sems)
    copies[0].start()
    copies[1].start()
    n, hidden = hid_ref.shape
    r = lax.broadcasted_iota(jnp.int32, (n, 1), 0)
    c = lax.broadcasted_iota(jnp.int32, (n, 2 * n), 1)
    at = (r // cap) * (2 * cap) + r % cap
    arrival.wait()
    last.start()
    for copy in copies[2:]:
        copy.start()
    got = got_ref[...]
    x = dot(jnp.where(c == at, 1.0, 0.0).astype(BF), got, ((1,), (0,))).astype(BF)
    dy = dot(jnp.where(c == at + cap, 1.0, 0.0).astype(BF), got, ((1,), (0,))).astype(BF)
    for h in range(0, hidden, STEP):
        copies[2 * h // STEP].wait()
        g = dot(x, wi_ref[:, h : h + STEP], ((1,), (0,)))
        copies[2 * h // STEP + 1].wait()
        u = dot(x, wi_ref[:, hidden + h : hidden + h + STEP], ((1,), (0,)))
        sig = jax.nn.sigmoid(g)
        swish = g * sig
        hid_ref[:, h : h + STEP] = (swish * u).astype(BF)
        if h == 0:
            last.wait()
        dh = dot(dy, wo_ref[:, h : h + STEP], ((1,), (0,)))
        da_ref[:, h : h + STEP] = (dh * u * sig * (1.0 + g * (1.0 - sig))).astype(BF)
        da_ref[:, hidden + h : hidden + h + STEP] = (dh * swish).astype(BF)
    y = dot(hid_ref[...], wo_ref[...], ((1,), (1,)))
    y_ref[...] = y.reshape(y_ref.shape).astype(BF)
    outs = [pltpu.make_async_copy(y_ref, y_hbm, sems.at[1])]
    outs[0].start()
    xt_ref[...] = jnp.transpose(x)
    dyt_ref[...] = jnp.transpose(dy)
    me = lax.axis_index("dp")
    me_y, me_x = me // RING, me % RING
    block = x.shape[1] // RING
    share = block // RING
    cuts = half_columns(hidden)
    for j in range(RING):
        y_at = (me_y + j) % RING
        rows = pl.ds(pl.multiple_of(y_at * block, block), block)
        for half, pieces in enumerate((a, b)):
            first = cuts[0] + hidden if half else 0
            outs_at = slice(cuts[0], hidden) if half else slice(0, cuts[0])
            cols = hidden + cuts[half]
            acc_ref[j, :, first : first + hidden] = dot(
                xt_ref[rows, :], da_ref[:, half * hidden : (half + 1) * hidden], ((1,), (0,))
            ).astype(BF)
            acc_ref[j, :, first + hidden : first + cols] = dot(
                dyt_ref[rows, :], hid_ref[:, outs_at], ((1,), (0,))
            ).astype(BF)
            for k in range(RING):
                if half == 0:
                    at = pl.multiple_of(((me_x + k) % RING) * share, share)
                    target = pieces[k].at[y_at]
                else:
                    at = k * share
                    target = pieces[j].at[k]
                source = acc_ref.at[j, pl.ds(at, share), pl.ds(first, cols)]
                outs.append(pltpu.make_async_copy(source, target, out_sems.at[half, j, k]))
                outs[-1].start()
    for copy in outs:
        copy.wait()


def middle_kernel(axis, *refs):
    parts, outs = refs[:RING], refs[RING:]
    me = lax.axis_index("dp")
    me = me // RING if axis == 0 else me % RING
    for t in range(RING):
        at = (me + t) % RING
        total = parts[0][at].astype(F32)
        for part in parts[1:]:
            total = total + part[at].astype(F32)
        cols = total.shape[1]
        outs[t][:, :cols] = total.astype(outs[t].dtype)
        if cols < outs[t].shape[1]:
            outs[t][:, cols:] = jnp.zeros((total.shape[0], outs[t].shape[1] - cols), outs[t].dtype)


def last_kernel(*refs):
    a, b = refs[:RING], refs[RING : 2 * RING]
    back_ref, pos_ref, g_ref, y_ref, in_ref, out_ref = refs[2 * RING :]
    half_in, few = in_ref.shape[1] // 2, half_columns(out_ref.shape[1])[0]
    for k, parts in enumerate((a, b)):
        total = parts[0][...]
        for part in parts[1:]:
            total = total + part[...].astype(F32)
        in_ref[:, k * half_in : (k + 1) * half_in] = total[:, :half_in]
        if k == 0:
            out_ref[:, :few] = total[:, half_in : half_in + few]
        else:
            out_ref[:, few:] = total[:, half_in:]
    tok = y_ref.shape[0]
    experts, cap, width = back_ref.shape
    g = jnp.transpose(jnp.broadcast_to(g_ref[...], (tok, tok)))[:, :1]
    rows = lax.broadcasted_iota(jnp.int32, (experts * cap, tok), 0)
    placing = jnp.where(rows == pos_ref[...], 1.0, 0.0).astype(BF)
    back = back_ref[...].astype(F32).reshape(experts * cap, width).astype(BF)
    y_ref[...] = (g * dot(placing, back, ((0,), (0,)))).astype(BF)


def on_device(latent, cotangent, routes, gates, w_in, w_out):
    n_experts = lax.axis_size("expert")
    tok, width = latent.shape
    hidden = w_out.shape[2]
    cap = max(2, 2 * tok // n_experts)
    rows = n_experts * cap
    gate_row = gates.reshape(1, tok)

    send, pos = call(
        functools.partial(place_kernel, cap),
        [((2 * rows, width), BF), ((1, tok), jnp.int32)],
        4 * rows * tok * width * 2, 4 * MIB, 4, hbm=4, vmem=62,
        scratch=[
            pltpu.VMEM((tok, width), BF),
            pltpu.VMEM((tok, width), BF),
            pltpu.VMEM((1, tok), jnp.int32),
            pltpu.VMEM((1, tok), F32),
            pltpu.SemaphoreType.DMA((4,)),
        ],
    )(latent, cotangent, routes.reshape(1, tok), gate_row)
    got = lax.all_to_all(
        send.reshape(n_experts, 2 * cap, width), "expert", split_axis=0, concat_axis=0, tiled=True
    ).reshape(2 * rows, width)

    share = width // (RING * RING)
    cols = [hidden + few for few in half_columns(hidden)]
    y_buf, *parts = call(
        functools.partial(expert_kernel, cap),
        [((n_experts, cap, width), BF)] + [((RING, share, c), BF) for c in cols for _ in range(RING)],
        2 * rows * width * hidden * 8, 16 * MIB, 3, hbm=3, vmem=58, out_hbm=True,
        scratch=[
            pltpu.VMEM((width, 2 * hidden), BF),
            pltpu.VMEM((width, hidden), BF),
            pltpu.VMEM((2 * rows, width), BF),
            pltpu.VMEM((n_experts, cap, width), BF),
            pltpu.VMEM((rows, hidden), BF),
            pltpu.VMEM((rows, 2 * hidden), BF),
            pltpu.VMEM((width, rows), BF),
            pltpu.VMEM((width, rows), BF),
            pltpu.VMEM((RING, width // RING, sum(cols)), BF),
            pltpu.SemaphoreType.DMA((2 * hidden // STEP + 1,)),
            pltpu.SemaphoreType.DMA((2,)),
            pltpu.SemaphoreType.DMA((2, RING, RING)),
        ],
    )(w_in[0], w_out[0], got)
    back = lax.all_to_all(y_buf, "expert", split_axis=0, concat_axis=0, tiled=True)

    def shift(v, dy, dx):
        ring = range(RING)
        pairs = [
            (RING * y + x, RING * ((y + dy) % RING) + (x + dx) % RING) for y in ring for x in ring
        ]
        return lax.ppermute(v, "dp", pairs)

    a, b = parts[:RING], parts[RING:]
    for k in range(1, RING):
        a[k] = shift(a[k], 0, k)
        b[k] = shift(b[k], k, 0)
    ends = []
    for axis, half in enumerate((a, b)):
        c = max(cols)
        mids = call(
            functools.partial(middle_kernel, axis),
            [((share, c), F32)] + [((share, c), BF)] * (RING - 1),
            8 * MIB, 5 * MIB, RING,
        )(half[0], half[2], half[1], half[3])
        far = [shift(mids[t], t, 0) if axis == 0 else shift(mids[t], 0, t) for t in (2, 1, 3)]
        ends += [mids[0]] + far
    output, grad_in, grad_out = call(
        last_kernel,
        [((tok, width), BF), ((share, 2 * hidden), F32), ((share, hidden), F32)],
        2 * rows * tok * width, 5 * MIB, 2 * RING + 3,
    )(*ends, back, pos, gate_row)
    return output, grad_in[None], grad_out[None]


def solution(mesh):
    tokens = P(("dp", "expert"), None)
    return jax.shard_map(
        on_device,
        mesh=mesh,
        in_specs=(tokens,) * 4 + (P("expert", None, None),) * 2,
        out_specs=(tokens, P("expert", "dp", None), P("expert", "dp", None)),
        check_vma=False,
    )
```

```python
import functools
import jax
import jax.numpy as jnp
from jax import lax
from jax.experimental import pallas as pl
from jax.experimental.pallas import tpu as pltpu
from jax.sharding import PartitionSpec as P

BF = jnp.bfloat16
F32 = jnp.float32
MIB = 1 << 20
RING = 4


def call(body, outs, flops, moved, n_in, vmem=12, scratch=(), hbm=0, out_hbm=False):
    vm = pl.BlockSpec(memory_space=pltpu.VMEM)
    far = pl.BlockSpec(memory_space=pltpu.HBM)
    return pl.pallas_call(
        body,
        out_shape=[jax.ShapeDtypeStruct(s, t) for s, t in outs],
        in_specs=[far] * hbm + [vm] * (n_in - hbm),
        out_specs=[far if out_hbm else vm] * len(outs),
        scratch_shapes=list(scratch),
        compiler_params=pltpu.CompilerParams(vmem_limit_bytes=vmem * MIB),
        cost_estimate=pl.CostEstimate(flops=flops, bytes_accessed=moved, transcendentals=0),
    )


def dot(a, b, dims):
    return lax.dot_general(a, b, (dims, ((), ())), preferred_element_type=F32)


def place_kernel(cap, x_hbm, c_hbm, r_hbm, g_hbm, send_ref, pos_ref, x_ref, c_ref, r_ref, g_ref, sems):
    pairs = ((r_hbm, r_ref), (g_hbm, g_ref), (x_hbm, x_ref), (c_hbm, c_ref))
    copies = [pltpu.make_async_copy(a, b, sems.at[i]) for i, (a, b) in enumerate(pairs)]
    for copy in copies:
        copy.start()
    for copy in copies:
        copy.wait()
    tok = x_ref.shape[0]
    r = jnp.broadcast_to(r_ref[...], (tok, tok))
    g = jnp.transpose(jnp.broadcast_to(g_ref[...], (tok, tok)))[:, :1]
    row = lax.broadcasted_iota(jnp.int32, (tok, tok), 0)
    col = lax.broadcasted_iota(jnp.int32, (tok, tok), 1)
    same = jnp.where((jnp.transpose(r) == r) & (row < col), 1, 0)
    slot = jnp.sum(same, axis=0, keepdims=True)
    route = r_ref[...]
    pos_ref[...] = route * cap + slot
    at = route * (2 * cap) + slot
    at = jnp.concatenate([at, at + cap], axis=1)
    rows = lax.broadcasted_iota(jnp.int32, (send_ref.shape[0], 2 * tok), 0)
    placing = jnp.where(rows == at, 1.0, 0.0).astype(BF)
    dy = (g * c_ref[...].astype(F32)).astype(BF)
    both = jnp.concatenate([x_ref[...], dy], axis=0)
    send_ref[...] = dot(placing, both, ((1,), (0,))).astype(BF)


STEP = 512


def weight_copies(wi_hbm, wo_hbm, wi_ref, wo_ref, sems):
    hidden = wo_hbm.shape[1]
    pieces = [pl.ds(at, STEP) for h in range(0, hidden, STEP) for at in (h, hidden + h)]
    copies = [
        pltpu.make_async_copy(wi_hbm.at[:, cols], wi_ref.at[:, cols], sems.at[i])
        for i, cols in enumerate(pieces)
    ]
    last = pltpu.make_async_copy(wo_hbm, wo_ref, sems.at[len(copies)])
    return copies, last


def half_columns(hidden):
    return hidden // 2, hidden // 2


def expert_kernel(cap, wi_hbm, wo_hbm, got_hbm, y_hbm, *refs):
    a, b = refs[:RING], refs[RING : 2 * RING]
    wi_ref, wo_ref, got_ref, y_ref, hid_ref, da_ref, xt_ref, dyt_ref, acc_ref, w_sems, sems, out_sems = refs[2 * RING :]
    arrival = pltpu.make_async_copy(got_hbm, got_ref, sems.at[0])
    arrival.start()
    copies, last = weight_copies(wi_hbm, wo_hbm, wi_ref, wo_ref, w_sems)
    copies[0].start()
    copies[1].start()
    n, hidden = hid_ref.shape
    r = lax.broadcasted_iota(jnp.int32, (n, 1), 0)
    c = lax.broadcasted_iota(jnp.int32, (n, 2 * n), 1)
    at = (r // cap) * (2 * cap) + r % cap
    arrival.wait()
    last.start()
    for copy in copies[2:]:
        copy.start()
    got = got_ref[...]
    x = dot(jnp.where(c == at, 1.0, 0.0).astype(BF), got, ((1,), (0,))).astype(BF)
    dy = dot(jnp.where(c == at + cap, 1.0, 0.0).astype(BF), got, ((1,), (0,))).astype(BF)
    for h in range(0, hidden, STEP):
        copies[2 * h // STEP].wait()
        g = dot(x, wi_ref[:, h : h + STEP], ((1,), (0,)))
        copies[2 * h // STEP + 1].wait()
        u = dot(x, wi_ref[:, hidden + h : hidden + h + STEP], ((1,), (0,)))
        sig = jax.nn.sigmoid(g)
        swish = g * sig
        hid_ref[:, h : h + STEP] = (swish * u).astype(BF)
        if h == 0:
            last.wait()
        dh = dot(dy, wo_ref[:, h : h + STEP], ((1,), (0,)))
        da_ref[:, h : h + STEP] = (dh * u * sig * (1.0 + g * (1.0 - sig))).astype(BF)
        da_ref[:, hidden + h : hidden + h + STEP] = (dh * swish).astype(BF)
    y = dot(hid_ref[...], wo_ref[...], ((1,), (1,)))
    y_ref[...] = y.reshape(y_ref.shape).astype(BF)
    outs = [pltpu.make_async_copy(y_ref, y_hbm, sems.at[1])]
    outs[0].start()
    xt_ref[...] = jnp.transpose(x)
    dyt_ref[...] = jnp.transpose(dy)
    me = lax.axis_index("dp")
    me_y, me_x = me // RING, me % RING
    block = x.shape[1] // RING
    share = block // RING
    cuts = half_columns(hidden)
    for j in range(RING):
        y_at = (me_y + j) % RING
        rows = pl.ds(pl.multiple_of(y_at * block, block), block)
        for half, pieces in enumerate((a, b)):
            first = cuts[0] + hidden if half else 0
            outs_at = slice(cuts[0], hidden) if half else slice(0, cuts[0])
            cols = hidden + cuts[half]
            acc_ref[j, :, first : first + hidden] = dot(
                xt_ref[rows, :], da_ref[:, half * hidden : (half + 1) * hidden], ((1,), (0,))
            ).astype(BF)
            acc_ref[j, :, first + hidden : first + cols] = dot(
                dyt_ref[rows, :], hid_ref[:, outs_at], ((1,), (0,))
            ).astype(BF)
            for k in range(RING):
                if half == 0:
                    at = pl.multiple_of(((me_x + k) % RING) * share, share)
                    target = pieces[k].at[y_at]
                else:
                    at = k * share
                    target = pieces[j].at[k]
                source = acc_ref.at[j, pl.ds(at, share), pl.ds(first, cols)]
                outs.append(pltpu.make_async_copy(source, target, out_sems.at[half, j, k]))
                outs[-1].start()
    for copy in outs:
        copy.wait()


def middle_kernel(axis, *refs):
    parts, outs = refs[:RING], refs[RING:]
    me = lax.axis_index("dp")
    me = me // RING if axis == 0 else me % RING
    for t in range(RING):
        at = (me + t) % RING
        total = parts[0][at].astype(F32)
        for part in parts[1:]:
            total = total + part[at].astype(F32)
        outs[t][...] = total.astype(outs[t].dtype)


def last_kernel(*refs):
    a, b = refs[:RING], refs[RING : 2 * RING]
    back_ref, pos_ref, g_ref, y_ref, in_ref, out_ref = refs[2 * RING :]
    half_in, few = in_ref.shape[1] // 2, half_columns(out_ref.shape[1])[0]
    for k, parts in enumerate((a, b)):
        total = parts[0][...]
        for part in parts[1:]:
            total = total + part[...].astype(F32)
        in_ref[:, k * half_in : (k + 1) * half_in] = total[:, :half_in]
        if k == 0:
            out_ref[:, :few] = total[:, half_in : half_in + few]
        else:
            out_ref[:, few:] = total[:, half_in:]
    tok = y_ref.shape[0]
    experts, cap, width = back_ref.shape
    g = jnp.transpose(jnp.broadcast_to(g_ref[...], (tok, tok)))[:, :1]
    rows = lax.broadcasted_iota(jnp.int32, (experts * cap, tok), 0)
    placing = jnp.where(rows == pos_ref[...], 1.0, 0.0).astype(BF)
    back = back_ref[...].astype(F32).reshape(experts * cap, width).astype(BF)
    y_ref[...] = (g * dot(placing, back, ((0,), (0,)))).astype(BF)


def on_device(latent, cotangent, routes, gates, w_in, w_out):
    n_experts = lax.axis_size("expert")
    tok, width = latent.shape
    hidden = w_out.shape[2]
    cap = max(2, 2 * tok // n_experts)
    rows = n_experts * cap
    gate_row = gates.reshape(1, tok)

    send, pos = call(
        functools.partial(place_kernel, cap),
        [((2 * rows, width), BF), ((1, tok), jnp.int32)],
        4 * rows * tok * width * 2, 4 * MIB, 4, hbm=4, vmem=62,
        scratch=[
            pltpu.VMEM((tok, width), BF),
            pltpu.VMEM((tok, width), BF),
            pltpu.VMEM((1, tok), jnp.int32),
            pltpu.VMEM((1, tok), F32),
            pltpu.SemaphoreType.DMA((4,)),
        ],
    )(latent, cotangent, routes.reshape(1, tok), gate_row)
    got = lax.all_to_all(
        send.reshape(n_experts, 2 * cap, width), "expert", split_axis=0, concat_axis=0, tiled=True
    ).reshape(2 * rows, width)

    share = width // (RING * RING)
    cols = [hidden + few for few in half_columns(hidden)]
    y_buf, *parts = call(
        functools.partial(expert_kernel, cap),
        [((n_experts, cap, width), BF)] + [((RING, share, c), BF) for c in cols for _ in range(RING)],
        2 * rows * width * hidden * 8, 16 * MIB, 3, hbm=3, vmem=58, out_hbm=True,
        scratch=[
            pltpu.VMEM((width, 2 * hidden), BF),
            pltpu.VMEM((width, hidden), BF),
            pltpu.VMEM((2 * rows, width), BF),
            pltpu.VMEM((n_experts, cap, width), BF),
            pltpu.VMEM((rows, hidden), BF),
            pltpu.VMEM((rows, 2 * hidden), BF),
            pltpu.VMEM((width, rows), BF),
            pltpu.VMEM((width, rows), BF),
            pltpu.VMEM((RING, width // RING, sum(cols)), BF),
            pltpu.SemaphoreType.DMA((2 * hidden // STEP + 1,)),
            pltpu.SemaphoreType.DMA((2,)),
            pltpu.SemaphoreType.DMA((2, RING, RING)),
        ],
    )(w_in[0], w_out[0], got)
    back = lax.all_to_all(y_buf, "expert", split_axis=0, concat_axis=0, tiled=True)

    def shift(v, dy, dx):
        ring = range(RING)
        pairs = [
            (RING * y + x, RING * ((y + dy) % RING) + (x + dx) % RING) for y in ring for x in ring
        ]
        return lax.ppermute(v, "dp", pairs)

    a, b = parts[:RING], parts[RING:]
    for k in range(1, RING):
        a[k] = shift(a[k], 0, k)
        b[k] = shift(b[k], k, 0)
    ends = []
    for axis, half in enumerate((a, b)):
        c = cols[axis]
        mids = call(
            functools.partial(middle_kernel, axis),
            [((share, c), F32)] + [((share, c), BF)] * (RING - 1),
            8 * MIB, 5 * MIB, RING,
        )(half[0], *[half[k] for k in ((2, 1, 3), (1, 3, 2))[axis]])
        far = [shift(mids[t], t, 0) if axis == 0 else shift(mids[t], 0, t) for t in ((1, 3, 2), (2, 1, 3))[axis]]
        ends += [mids[0]] + far
    output, grad_in, grad_out = call(
        last_kernel,
        [((tok, width), BF), ((share, 2 * hidden), F32), ((share, hidden), F32)],
        2 * rows * tok * width, 5 * MIB, 2 * RING + 3,
    )(*ends, back, pos, gate_row)
    return output, grad_in[None], grad_out[None]


def solution(mesh):
    tokens = P(("dp", "expert"), None)
    return jax.shard_map(
        on_device,
        mesh=mesh,
        in_specs=(tokens,) * 4 + (P("expert", None, None),) * 2,
        out_specs=(tokens, P("expert", "dp", None), P("expert", "dp", None)),
        check_vma=False,
    )
```

```python
import functools
import jax
import jax.numpy as jnp
from jax import lax
from jax.experimental import pallas as pl
from jax.experimental.pallas import tpu as pltpu
from jax.sharding import PartitionSpec as P

BF = jnp.bfloat16
F32 = jnp.float32
MIB = 1 << 20
RING = 4


def call(body, outs, flops, moved, n_in, vmem=12, scratch=(), hbm=0, out_hbm=False):
    vm = pl.BlockSpec(memory_space=pltpu.VMEM)
    far = pl.BlockSpec(memory_space=pltpu.HBM)
    return pl.pallas_call(
        body,
        out_shape=[jax.ShapeDtypeStruct(s, t) for s, t in outs],
        in_specs=[far] * hbm + [vm] * (n_in - hbm),
        out_specs=[far if out_hbm else vm] * len(outs),
        scratch_shapes=list(scratch),
        compiler_params=pltpu.CompilerParams(vmem_limit_bytes=vmem * MIB),
        cost_estimate=pl.CostEstimate(flops=flops, bytes_accessed=moved, transcendentals=0),
    )


def dot(a, b, dims):
    return lax.dot_general(a, b, (dims, ((), ())), preferred_element_type=F32)


def place_kernel(cap, x_hbm, c_hbm, r_hbm, g_hbm, send_ref, pos_ref, x_ref, c_ref, r_ref, g_ref, sems):
    pairs = ((r_hbm, r_ref), (g_hbm, g_ref), (x_hbm, x_ref), (c_hbm, c_ref))
    copies = [pltpu.make_async_copy(a, b, sems.at[i]) for i, (a, b) in enumerate(pairs)]
    for copy in copies:
        copy.start()
    for copy in copies[:2]:
        copy.wait()
    tok = x_ref.shape[0]
    r = jnp.broadcast_to(r_ref[...], (tok, tok))
    g = jnp.transpose(jnp.broadcast_to(g_ref[...], (tok, tok)))[:, :1]
    row = lax.broadcasted_iota(jnp.int32, (tok, tok), 0)
    col = lax.broadcasted_iota(jnp.int32, (tok, tok), 1)
    same = jnp.where((jnp.transpose(r) == r) & (row < col), 1, 0)
    slot = jnp.sum(same, axis=0, keepdims=True)
    route = r_ref[...]
    pos_ref[...] = route * cap + slot
    at = route * (2 * cap) + slot
    at = jnp.concatenate([at, at + cap], axis=1)
    rows = lax.broadcasted_iota(jnp.int32, (send_ref.shape[0], 2 * tok), 0)
    placing = jnp.where(rows == at, 1.0, 0.0).astype(BF)
    for copy in copies[2:]:
        copy.wait()
    dy = (g * c_ref[...].astype(F32)).astype(BF)
    both = jnp.concatenate([x_ref[...], dy], axis=0)
    send_ref[...] = dot(placing, both, ((1,), (0,))).astype(BF)


STEP = 512


def weight_copies(wi_hbm, wo_hbm, wi_ref, wo_ref, sems):
    hidden = wo_hbm.shape[1]
    pieces = [pl.ds(at, STEP) for h in range(0, hidden, STEP) for at in (h, hidden + h)]
    copies = [
        pltpu.make_async_copy(wi_hbm.at[:, cols], wi_ref.at[:, cols], sems.at[i])
        for i, cols in enumerate(pieces)
    ]
    last = pltpu.make_async_copy(wo_hbm, wo_ref, sems.at[len(copies)])
    return copies, last


def half_columns(hidden):
    return hidden // 2, hidden // 2


def expert_kernel(cap, wi_hbm, wo_hbm, got_hbm, y_hbm, *refs):
    a, b = refs[:RING], refs[RING : 2 * RING]
    wi_ref, wo_ref, got_ref, y_ref, hid_ref, da_ref, xt_ref, dyt_ref, acc_ref, w_sems, sems, out_sems = refs[2 * RING :]
    arrival = pltpu.make_async_copy(got_hbm, got_ref, sems.at[0])
    arrival.start()
    copies, last = weight_copies(wi_hbm, wo_hbm, wi_ref, wo_ref, w_sems)
    copies[0].start()
    copies[1].start()
    n, hidden = hid_ref.shape
    r = lax.broadcasted_iota(jnp.int32, (n, 1), 0)
    c = lax.broadcasted_iota(jnp.int32, (n, 2 * n), 1)
    at = (r // cap) * (2 * cap) + r % cap
    pick_x = jnp.where(c == at, 1.0, 0.0).astype(BF)
    pick_dy = jnp.where(c == at + cap, 1.0, 0.0).astype(BF)
    arrival.wait()
    last.start()
    for copy in copies[2:]:
        copy.start()
    got = got_ref[...]
    x = dot(pick_x, got, ((1,), (0,))).astype(BF)
    dy = dot(pick_dy, got, ((1,), (0,))).astype(BF)
    for h in range(0, hidden, STEP):
        copies[2 * h // STEP].wait()
        g = dot(x, wi_ref[:, h : h + STEP], ((1,), (0,)))
        copies[2 * h // STEP + 1].wait()
        u = dot(x, wi_ref[:, hidden + h : hidden + h + STEP], ((1,), (0,)))
        sig = jax.nn.sigmoid(g)
        swish = g * sig
        hid_ref[:, h : h + STEP] = (swish * u).astype(BF)
        if h == 0:
            last.wait()
        dh = dot(dy, wo_ref[:, h : h + STEP], ((1,), (0,)))
        da_ref[:, h : h + STEP] = (dh * u * sig * (1.0 + g * (1.0 - sig))).astype(BF)
        da_ref[:, hidden + h : hidden + h + STEP] = (dh * swish).astype(BF)
    y = dot(hid_ref[...], wo_ref[...], ((1,), (1,)))
    y_ref[...] = y.reshape(y_ref.shape).astype(BF)
    outs = [pltpu.make_async_copy(y_ref, y_hbm, sems.at[1])]
    outs[0].start()
    xt_ref[...] = jnp.transpose(x)
    dyt_ref[...] = jnp.transpose(dy)
    me = lax.axis_index("dp")
    me_y, me_x = me // RING, me % RING
    block = x.shape[1] // RING
    share = block // RING
    cuts = half_columns(hidden)
    for j in range(RING):
        y_at = (me_y + j) % RING
        rows = pl.ds(pl.multiple_of(y_at * block, block), block)
        for half, pieces in enumerate((a, b)):
            first = cuts[0] + hidden if half else 0
            outs_at = slice(cuts[0], hidden) if half else slice(0, cuts[0])
            cols = hidden + cuts[half]
            acc_ref[j, :, first : first + hidden] = dot(
                xt_ref[rows, :], da_ref[:, half * hidden : (half + 1) * hidden], ((1,), (0,))
            ).astype(BF)
            acc_ref[j, :, first + hidden : first + cols] = dot(
                dyt_ref[rows, :], hid_ref[:, outs_at], ((1,), (0,))
            ).astype(BF)
            for k in range(RING):
                if half == 0:
                    at = pl.multiple_of(((me_x + k) % RING) * share, share)
                    target = pieces[k].at[y_at]
                else:
                    at = k * share
                    target = pieces[j].at[k]
                source = acc_ref.at[j, pl.ds(at, share), pl.ds(first, cols)]
                outs.append(pltpu.make_async_copy(source, target, out_sems.at[half, j, k]))
                outs[-1].start()
    for copy in outs:
        copy.wait()


def middle_kernel(axis, *refs):
    parts, outs = refs[:RING], refs[RING:]
    me = lax.axis_index("dp")
    me = me // RING if axis == 0 else me % RING
    for t in range(RING):
        at = (me + t) % RING
        total = parts[0][at].astype(F32)
        for part in parts[1:]:
            total = total + part[at].astype(F32)
        outs[t][...] = total.astype(outs[t].dtype)


def last_kernel(*refs):
    a, b = refs[:RING], refs[RING : 2 * RING]
    back_ref, pos_ref, g_ref, y_ref, in_ref, out_ref = refs[2 * RING :]
    half_in, few = in_ref.shape[1] // 2, half_columns(out_ref.shape[1])[0]
    for k, parts in enumerate((a, b)):
        total = parts[0][...]
        for part in parts[1:]:
            total = total + part[...].astype(F32)
        in_ref[:, k * half_in : (k + 1) * half_in] = total[:, :half_in]
        if k == 0:
            out_ref[:, :few] = total[:, half_in : half_in + few]
        else:
            out_ref[:, few:] = total[:, half_in:]
    tok = y_ref.shape[0]
    experts, cap, width = back_ref.shape
    g = jnp.transpose(jnp.broadcast_to(g_ref[...], (tok, tok)))[:, :1]
    rows = lax.broadcasted_iota(jnp.int32, (experts * cap, tok), 0)
    placing = jnp.where(rows == pos_ref[...], 1.0, 0.0).astype(BF)
    back = back_ref[...].astype(F32).reshape(experts * cap, width).astype(BF)
    y_ref[...] = (g * dot(placing, back, ((0,), (0,)))).astype(BF)


def on_device(latent, cotangent, routes, gates, w_in, w_out):
    n_experts = lax.axis_size("expert")
    tok, width = latent.shape
    hidden = w_out.shape[2]
    cap = max(2, 2 * tok // n_experts)
    rows = n_experts * cap
    gate_row = gates.reshape(1, tok)

    send, pos = call(
        functools.partial(place_kernel, cap),
        [((2 * rows, width), BF), ((1, tok), jnp.int32)],
        4 * rows * tok * width * 2, 4 * MIB, 4, hbm=4, vmem=62,
        scratch=[
            pltpu.VMEM((tok, width), BF),
            pltpu.VMEM((tok, width), BF),
            pltpu.VMEM((1, tok), jnp.int32),
            pltpu.VMEM((1, tok), F32),
            pltpu.SemaphoreType.DMA((4,)),
        ],
    )(latent, cotangent, routes.reshape(1, tok), gate_row)
    got = lax.all_to_all(
        send.reshape(n_experts, 2 * cap, width), "expert", split_axis=0, concat_axis=0, tiled=True
    ).reshape(2 * rows, width)

    share = width // (RING * RING)
    cols = [hidden + few for few in half_columns(hidden)]
    y_buf, *parts = call(
        functools.partial(expert_kernel, cap),
        [((n_experts, cap, width), BF)] + [((RING, share, c), BF) for c in cols for _ in range(RING)],
        2 * rows * width * hidden * 8, 16 * MIB, 3, hbm=3, vmem=58, out_hbm=True,
        scratch=[
            pltpu.VMEM((width, 2 * hidden), BF),
            pltpu.VMEM((width, hidden), BF),
            pltpu.VMEM((2 * rows, width), BF),
            pltpu.VMEM((n_experts, cap, width), BF),
            pltpu.VMEM((rows, hidden), BF),
            pltpu.VMEM((rows, 2 * hidden), BF),
            pltpu.VMEM((width, rows), BF),
            pltpu.VMEM((width, rows), BF),
            pltpu.VMEM((RING, width // RING, sum(cols)), BF),
            pltpu.SemaphoreType.DMA((2 * hidden // STEP + 1,)),
            pltpu.SemaphoreType.DMA((2,)),
            pltpu.SemaphoreType.DMA((2, RING, RING)),
        ],
    )(w_in[0], w_out[0], got)
    back = lax.all_to_all(y_buf, "expert", split_axis=0, concat_axis=0, tiled=True)

    def shift(v, dy, dx):
        ring = range(RING)
        pairs = [
            (RING * y + x, RING * ((y + dy) % RING) + (x + dx) % RING) for y in ring for x in ring
        ]
        return lax.ppermute(v, "dp", pairs)

    a, b = parts[:RING], parts[RING:]
    for k in range(1, RING):
        a[k] = shift(a[k], 0, k)
        b[k] = shift(b[k], k, 0)
    ends = []
    for axis, half in enumerate((a, b)):
        c = cols[axis]
        mids = call(
            functools.partial(middle_kernel, axis),
            [((share, c), F32)] + [((share, c), BF)] * (RING - 1),
            8 * MIB, 5 * MIB, RING,
        )(half[0], *[half[k] for k in ((2, 1, 3), (1, 3, 2))[axis]])
        far = [shift(mids[t], t, 0) if axis == 0 else shift(mids[t], 0, t) for t in ((3, 1, 2), (2, 1, 3))[axis]]
        ends += [mids[0]] + far
    output, grad_in, grad_out = call(
        last_kernel,
        [((tok, width), BF), ((share, 2 * hidden), F32), ((share, hidden), F32)],
        2 * rows * tok * width, 5 * MIB, 2 * RING + 3,
    )(*ends, back, pos, gate_row)
    return output, grad_in[None], grad_out[None]


def solution(mesh):
    tokens = P(("dp", "expert"), None)
    return jax.shard_map(
        on_device,
        mesh=mesh,
        in_specs=(tokens,) * 4 + (P("expert", None, None),) * 2,
        out_specs=(tokens, P("expert", "dp", None), P("expert", "dp", None)),
        check_vma=False,
    )
```
